32 devices in a mesh: lat: 4 (over y, x), lon: 8 (over z, core).
Axes of the slice: x: 2, y: 2, z: 4, core: 2. Of those that a mesh axis runs over, the one named last changes fastest.
Arguments:
- analysis_fields: float32 [69, 384, 360], P(None, 'lat', 'lon'), may hold values from -6 to 6
- response_inphase: float32 [69, 180], replicated, may hold values from -5 to 5
- response_quadrature: float32 [69, 180], replicated, may hold values from -5 to 5
- entry_projection_matrix: float32 [69, 768], replicated, may hold values from -0.75 to 0.75
- exit_projection_matrix: float32 [768, 69], replicated, may hold values from -0.21875 to 0.21875
- radiance_op: float32 [69, 256], replicated, may hold values from -0.75 to 0.75
- inv_var: float32 [256], replicated, may hold values from 0.1 to 1
- observed: float32 [256, 1024, 128], P(None, ('lat', 'lon')), may hold values from -6 to 6
- cell_index: int32 [1024, 128], P(('lat', 'lon')), may hold values from 0 to 4319
- obs_mask: int32 [1024, 128], P(('lat', 'lon')), may hold values from 0 to 1, as said below
Outputs:
- gradient: float32 [69, 384, 360], P(None, 'lat', 'lon')
The draws below stay inside these ranges and needn't reach their ends.
Inputs may be any that keep to these rules, and one draw needn't show every extreme that they name: `obs_mask`: in every slot row the live slots come first: slot k is live when k is below the row's count of columns. In every draw one owner receives a full row of 128 columns from every source, and that owner is drawn from the seed.
All inputs are finite; a program needn't handle non-finite values.
Results may differ from the reference program's by a relative error of at most 0.0001.
Values sent between devices are 32-bit elements; how exact they have to be, the bound alone decides.
No kernel may reach another device: no remote copies, remote signals or barrier semaphores. Data moves between devices by JAX's collectives and lax.ppermute only.
A program may use at most 256 MiB of HBM per device.

```python
import math
import jax
import jax.numpy as jnp
from jax import lax

FIELD_QUANTITY = 69
NCH = 256
HID = 768
CAP = 128
PARALLEL_CIRCLES = 96
MERIDIAN_TOTAL = 45
NLAT = 384
NLON = 360
MODES = 180
CELLS_DEV = 4320
ROWS = 1024
N_LAT = 4
N_LON = 8
DEVICES = 32


def draw_obs_mask(key, part):
    first = jax.random.fold_in(key, 11)
    second = jax.random.fold_in(key, 12)
    lowest = max(1, CAP // 8)
    counts = jax.random.randint(first, (DEVICES, DEVICES), lowest, CAP + 1)
    full_owner = jax.random.randint(second, (), 0, DEVICES)
    owners = jnp.arange(DEVICES, dtype=jnp.int32)
    counts = jnp.where(owners[None, :] == full_owner, CAP, counts)
    slots = jnp.arange(CAP, dtype=jnp.int32)
    live = (slots[None, None, :] < counts[:, :, None]).astype(jnp.int32)
    return live.reshape(DEVICES * DEVICES, CAP)


def place_ends(result, key, least, high):
    extent = result.shape
    index_at = [jax.random.randint(jax.random.fold_in(key, axis), (), 0, extent[axis]) for axis in range(len(extent))]
    result = result.at[tuple(index_at)].set(least)
    longest = extent.index(max(extent))
    index_at[longest] = (index_at[longest] + 1) % extent[longest]
    return result.at[tuple(index_at)].set(high)


def steps_of(key, dims, shards, low, high):
    level = 1.0
    for position, parts in shards:
        heights = jax.random.uniform(jax.random.fold_in(jax.random.fold_in(key, 6), position), (parts,), jnp.float32, low / len(shards), high / len(shards))
        level = level * jnp.repeat(jnp.exp(heights), dims[position] // parts).reshape((-1,) + (1,) * (len(dims) - 1 - position))
    return level


def noise(stream_key, shape, width, most, cuts=(), held_as=jnp.bfloat16):
    result = jax.random.normal(stream_key, shape, jnp.float32) * width
    if len(cuts) > 0:
        result = steps_of(stream_key, shape, cuts, -0.22, 0.18) * result
    return jnp.clip(result, min=-most, max=most).astype(held_as)


def setup_inputs(seed: int = 0) -> dict:
    streams_of = jax.random.split(jax.random.key(seed), 11)
    return {
        "analysis_fields": noise(streams_of[0], (FIELD_QUANTITY, NLAT, NLON), 1.0, 6.0, ((1, 4), (2, 8)), jnp.float32),
        "response_inphase": noise(streams_of[1], (FIELD_QUANTITY, MODES), 1.0, 5.0, (), jnp.float32),
        "response_quadrature": noise(streams_of[2], (FIELD_QUANTITY, MODES), 1.0, 5.0, (), jnp.float32),
        "entry_projection_matrix": noise(streams_of[3], (FIELD_QUANTITY, HID), FIELD_QUANTITY ** -0.5, 0.75, (), jnp.float32),
        "exit_projection_matrix": noise(streams_of[4], (HID, FIELD_QUANTITY), HID ** -0.5, 0.21875, (), jnp.float32),
        "radiance_op": noise(streams_of[5], (FIELD_QUANTITY, NCH), FIELD_QUANTITY ** -0.5, 0.75, (), jnp.float32),
        "inv_var": jnp.clip(jnp.exp(jax.random.uniform(streams_of[6], (NCH,), jnp.float32, math.log(0.1), math.log(1.0))), 0.1, 1.0),
        "observed": noise(streams_of[7], (NCH, ROWS, CAP), 1.0, 6.0, ((1, 32),), jnp.float32),
        "cell_index": place_ends(jax.random.randint(streams_of[8], (ROWS, CAP), 0, CELLS_DEV), jax.random.fold_in(streams_of[8], 1), 0, CELLS_DEV - 1).astype(jnp.int32),
        "obs_mask": draw_obs_mask(jax.random.fold_in(streams_of[10], 71), 0),
    }


def spectral_filter(field, response_inphase, response_quadrature):
    nlon = field.shape[-1]
    modes = nlon // 2
    spectrum = jnp.fft.rfft(field, axis=-1)[..., :modes]
    gain = response_inphase[:, None, :] + 1j * response_quadrature[:, None, :]
    return jnp.fft.irfft(gain * spectrum, n=nlon, axis=-1)

def channel_perceptron(mixed_state, entry_projection_matrix, exit_projection_matrix):
    raveled_vector = mixed_state.reshape(mixed_state.shape[0], -1)
    hidden = jax.nn.gelu(jnp.dot(entry_projection_matrix.T, raveled_vector, precision=lax.Precision.HIGHEST), approximate=True)
    out = raveled_vector + jnp.dot(exit_projection_matrix.T, hidden, precision=lax.Precision.HIGHEST)
    return out.reshape(mixed_state.shape)

def propagate_dynamics(field, response_inphase, response_quadrature, entry_projection_matrix, exit_projection_matrix):
    mixed_state = field + spectral_filter(field, response_inphase, response_quadrature)
    return channel_perceptron(mixed_state, entry_projection_matrix, exit_projection_matrix)

def reference(analysis_fields, response_inphase, response_quadrature, entry_projection_matrix, exit_projection_matrix, radiance_op, inv_var, observed, cell_index, obs_mask):
    predicted_fields, reverse_derivative_map = jax.vjp(lambda sensitivity_vector: propagate_dynamics(sensitivity_vector, response_inphase, response_quadrature, entry_projection_matrix, exit_projection_matrix), analysis_fields)
    devices = N_LAT * N_LON
    domain_tiles = predicted_fields.reshape(FIELD_QUANTITY, N_LAT, PARALLEL_CIRCLES, N_LON, MERIDIAN_TOTAL).transpose(0, 1, 3, 2, 4)
    domain_tiles = domain_tiles.reshape(FIELD_QUANTITY, devices * CELLS_DEV)
    owner = (jnp.arange(devices * devices, dtype=jnp.int32) % devices)[:, None]
    global_index = (owner * CELLS_DEV + cell_index).astype(jnp.int32)
    weights = obs_mask.astype(jnp.float32)

    def one_source(source, total):
        start = (source * devices).astype(jnp.int32)
        index = lax.dynamic_slice_in_dim(global_index, start, devices, 0)
        live = lax.dynamic_slice_in_dim(weights, start, devices, 0)
        seen = lax.dynamic_slice_in_dim(observed, start, devices, 1)
        values = domain_tiles[:, index]
        radiance = jnp.einsum('ck,cdn->kdn', radiance_op, values, precision=lax.Precision.HIGHEST)
        deviation = live[None] * inv_var[:, None, None] * (radiance - seen)
        adjoint = jnp.einsum('ck,kdn->cdn', radiance_op, deviation, precision=lax.Precision.HIGHEST)
        return total.at[:, index].add(adjoint)
    total = lax.fori_loop(jnp.int32(0), jnp.int32(devices), one_source, jnp.zeros_like(domain_tiles))
    forcing = total.reshape(FIELD_QUANTITY, N_LAT, N_LON, PARALLEL_CIRCLES, MERIDIAN_TOTAL).transpose(0, 1, 3, 2, 4)
    forcing = forcing.reshape(FIELD_QUANTITY, NLAT, NLON)
    return reverse_derivative_map(forcing)[0]
```

```python
import math

import jax
import jax.numpy as jnp
from jax import lax
from jax.sharding import PartitionSpec as P


def make_tables(nlon):
    modes = nlon // 2
    columns = jnp.arange(nlon, dtype=jnp.int32)
    waves = jnp.arange(modes, dtype=jnp.int32)
    phase = columns[:, None] * waves[None, :] % nlon
    angle = phase.astype(jnp.float32) * (2.0 * math.pi / nlon)
    cosine = jnp.cos(angle)
    sine = jnp.sin(angle)
    forward = jnp.concatenate([cosine, -sine], axis=1)
    weight = jnp.where(waves == 0, 1.0, 2.0).astype(jnp.float32) / nlon
    inverse = jnp.concatenate([(cosine * weight[None, :]).T, -(sine * weight[None, :]).T], axis=0)
    return (forward, inverse)


def channel_perceptron(mixed_state, entry_projection_matrix, exit_projection_matrix):
    raveled_vector = mixed_state.reshape(mixed_state.shape[0], -1)
    hidden = jax.nn.gelu(
        jnp.dot(entry_projection_matrix.T, raveled_vector, precision=lax.Precision.HIGH),
        approximate=True,
    )
    out = raveled_vector + jnp.dot(
        exit_projection_matrix.T, hidden, precision=lax.Precision.HIGH
    )
    return out.reshape(mixed_state.shape)


def send_requests(index):
    return lax.all_to_all(index, ("lat", "lon"), split_axis=0, concat_axis=0, tiled=True)


def send_adjoint(values):
    return lax.all_to_all(values, ("lat", "lon"), split_axis=1, concat_axis=1, tiled=True)


def local(
    analysis_fields,
    response_inphase,
    response_quadrature,
    entry_projection_matrix,
    exit_projection_matrix,
    radiance_op,
    inv_var,
    observed,
    cell_index,
    obs_mask,
):
    spectral_bands = analysis_fields.shape[0]
    nlon = analysis_fields.shape[2] * lax.axis_size("lon")
    modes = nlon // 2
    forward, inverse = make_tables(nlon)

    def spectral_filter(field):
        spectrum = jnp.einsum("crj,jm->crm", field, forward, precision=lax.Precision.HIGH)
        spec_real = spectrum[..., :modes]
        spec_imag = spectrum[..., modes:]
        gr = response_inphase[:, None, :]
        gi = response_quadrature[:, None, :]
        out_real = gr * spec_real - gi * spec_imag
        out_imag = gr * spec_imag + gi * spec_real
        joined = jnp.concatenate([out_real, out_imag], axis=-1)
        return jnp.einsum("crm,mj->crj", joined, inverse, precision=lax.Precision.HIGH)

    circles = lax.all_to_all(analysis_fields, "lon", split_axis=1, concat_axis=2, tiled=True)
    filtered, pull_filter = jax.vjp(spectral_filter, circles)
    shifted = lax.all_to_all(filtered, "lon", split_axis=2, concat_axis=1, tiled=True)
    mixed_state = analysis_fields + shifted
    predicted_fields, network_backprop = jax.vjp(
        lambda sensitivity_vector: channel_perceptron(
            sensitivity_vector, entry_projection_matrix, exit_projection_matrix
        ),
        mixed_state,
    )
    raveled_vector = predicted_fields.reshape(spectral_bands, -1)
    cell_count = raveled_vector.shape[1]
    key = jnp.where(obs_mask > 0, cell_index, -1)
    wanted = send_requests(key).reshape(-1)
    weighted_op = radiance_op * inv_var[None, :]
    normal = jnp.dot(weighted_op, radiance_op.T, precision=lax.Precision.HIGHEST)
    pulled = jnp.einsum("ck,kdn->cdn", weighted_op, observed, precision=lax.Precision.HIGH)
    arrived = send_adjoint(pulled).reshape(spectral_bands, -1)
    rounded = lax.reduce_precision(arrived, exponent_bits=8, mantissa_bits=7)
    upper = rounded.astype(jnp.bfloat16)
    lower = (arrived - rounded).astype(jnp.bfloat16)
    ones = jnp.ones((1, arrived.shape[1]), jnp.bfloat16)
    stacked = jnp.concatenate([upper, lower, ones], axis=0)
    cell_ids = jnp.arange(cell_count, dtype=jnp.int32)
    onehot = (wanted[:, None] == cell_ids[None, :]).astype(jnp.bfloat16)
    sums = jnp.dot(stacked, onehot, preferred_element_type=jnp.float32)
    pulled_cells = sums[:spectral_bands] + sums[spectral_bands : 2 * spectral_bands]
    count = sums[2 * spectral_bands :]
    cells = count * jnp.dot(normal, raveled_vector, precision=lax.Precision.HIGH) - pulled_cells
    forcing = cells.reshape(analysis_fields.shape)
    d_mixed = network_backprop(forcing)[0]
    circle_adjoint = lax.all_to_all(d_mixed, "lon", split_axis=1, concat_axis=2, tiled=True)
    d_circles = pull_filter(circle_adjoint)[0]
    returned = lax.all_to_all(d_circles, "lon", split_axis=2, concat_axis=1, tiled=True)
    return d_mixed + returned


def solution(mesh):
    return jax.shard_map(
        local,
        mesh=mesh,
        in_specs=(
            P(None, "lat", "lon"),
            P(),
            P(),
            P(),
            P(),
            P(),
            P(),
            P(None, ("lat", "lon"), None),
            P(("lat", "lon"), None),
            P(("lat", "lon"), None),
        ),
        out_specs=P(None, "lat", "lon"),
        check_vma=False,
    )
```

```python
import functools
import math

import jax
import jax.numpy as jnp
from jax import lax
from jax.experimental import pallas as pl
from jax.experimental.pallas import tpu as pltpu
from jax.sharding import PartitionSpec as P

VMEM_LIMIT = 56 * 1024 * 1024
CELL_TILE = 256
F32 = jnp.float32
BF16 = jnp.bfloat16


def round_up(value, unit):
    return -(-value // unit) * unit


class Plan:
    def __init__(self, variables, rows, lons, ring):
        self.variables = variables
        self.rows = rows
        self.lons = lons
        self.ring = ring
        self.pitch = round_up(variables, 8)
        self.lons_pad = round_up(lons, 16)
        self.full = variables // ring
        self.left = variables - self.full * ring
        self.left_lanes = -(-self.left * rows // ring)
        self.left_width = round_up(max(self.left_lanes * ring, 1), 128)
        self.lanes = self.full * rows + self.left_lanes
        self.lanes_pad = round_up(self.lanes, 128)
        self.tiles = self.lanes // 128
        self.rest = self.lanes - self.tiles * 128
        self.half = (lons + 1) // 2
        self.folded = 0 < self.rest <= 64
        tail = 0 if self.rest == 0 else (self.half if self.folded else lons)
        self.wire_rows = self.tiles * lons + tail
        self.cells = lons * rows
        self.cells_pad = round_up(self.cells, CELL_TILE)
        self.nlon = lons * ring
        self.modes = self.nlon // 2
        self.modes_pad = round_up(self.modes, 8)


def split(value):
    upper = value.astype(BF16)
    lower = (value - upper.astype(F32)).astype(BF16)
    return upper, lower


def mm(a, b):
    return jnp.dot(a, b, preferred_element_type=F32)


def put_wire(plan, ref, block):
    lons = plan.lons
    for t in range(plan.tiles):
        ref[t * lons : (t + 1) * lons, :] = block[:, t * 128 : (t + 1) * 128]
    if plan.rest == 0:
        return
    last = block[:, plan.tiles * 128 :]
    if plan.folded:
        last = jnp.concatenate([last[: plan.half, :64], last[lons - plan.half :, :64]], axis=1)
    ref[plan.tiles * lons :, :] = last


def get_wire(plan, ref):
    lons = plan.lons
    found = [ref[t * lons : (t + 1) * lons, :] for t in range(plan.tiles)]
    if plan.rest > 0:
        last = ref[plan.tiles * lons : plan.wire_rows, :]
        if plan.folded:
            again = pltpu.roll(last, 64, 1)
            last = jnp.concatenate([last, again[2 * plan.half - lons :]], axis=0)
        found.append(last)
    return found


def pack_blocks(plan, me, field_ref, out_refs):
    lons, rows = plan.lons, plan.rows

    def variable(c):
        return field_ref[pl.ds(c, lons, stride=plan.pitch), :][:, :rows]

    left = None
    if plan.left > 0:
        first = plan.full * plan.ring
        pieces = [variable(first + i) for i in range(plan.left)]
        spare = plan.left_width - plan.left * rows
        if spare > 0:
            pieces.append(jnp.zeros((lons, spare), F32))
        left = jnp.concatenate(pieces, axis=1)
    for k, out_ref in enumerate(out_refs):
        q = me ^ k
        pieces = [variable(q * plan.full + i) for i in range(plan.full)]
        if left is not None:
            shift = lax.rem(plan.left_width - q * plan.left_lanes, plan.left_width)
            pieces.append(pltpu.roll(left, shift, 1)[:, : plan.left_lanes])
        spare = plan.lanes_pad - plan.lanes
        if spare > 0:
            pieces.append(jnp.zeros((lons, spare), F32))
        put_wire(plan, out_ref, jnp.concatenate(pieces, axis=1))


def add_blocks(plan, me, field_ref, in_refs):
    lons, rows = plan.lons, plan.rows
    left = jnp.zeros((lons, plan.left_width), F32)
    lane = lax.broadcasted_iota(jnp.int32, (lons, plan.left_width), 1)
    for k, in_ref in enumerate(in_refs):
        q = me ^ k
        block = jnp.concatenate(get_wire(plan, in_ref), axis=1)
        for i in range(plan.full):
            at = pl.ds(q * plan.full + i, lons, stride=plan.pitch)
            piece = block[:, i * rows : (i + 1) * rows]
            field_ref[at, :] = field_ref[at, :] + jnp.pad(piece, ((0, 0), (0, 128 - rows)))
        if plan.left > 0:
            piece = block[:, plan.full * rows : plan.lanes]
            piece = jnp.pad(piece, ((0, 0), (0, plan.left_width - plan.left_lanes)))
            left = left + pltpu.roll(piece, q * plan.left_lanes, 1)
    for i in range(plan.left):
        at = pl.ds(plan.full * plan.ring + i, lons, stride=plan.pitch)
        piece = left[:, i * rows : (i + 1) * rows]
        field_ref[at, :] = field_ref[at, :] + jnp.pad(piece, ((0, 0), (0, 128 - rows)))


def load_field(plan, field_ref, source_ref):
    pad = jnp.zeros((plan.pitch, 128), F32)
    for j in range(plan.lons):
        field_ref[j * plan.pitch : (j + 1) * plan.pitch, :] = pad
        field_ref[j * plan.pitch : j * plan.pitch + plan.variables, : plan.rows] = source_ref[j]


def pack_kernel(plan, me_ref, state_ref, *rest):
    out_refs, field_ref = rest[:-1], rest[-1]
    load_field(plan, field_ref, state_ref)
    pack_blocks(plan, me_ref[0], field_ref, out_refs)


def filter_kernel(plan, fwd_hi, fwd_lo, inv_hi, inv_lo, gain_re, gain_im, *rest):
    ring = plan.ring
    in_refs, out_refs = rest[:ring], rest[ring : 2 * ring]
    hi_ref, lo_ref = rest[2 * ring :]
    lons, step = plan.lons, plan.lons_pad
    for k in range(ring):
        for t, tile in enumerate(get_wire(plan, in_refs[k])):
            tile = jnp.concatenate([tile, jnp.zeros((step - lons, 128), F32)], axis=0)
            upper, lower = split(tile)
            hi_ref[k * step : (k + 1) * step, t * 128 : (t + 1) * 128] = upper
            lo_ref[k * step : (k + 1) * step, t * 128 : (t + 1) * 128] = lower
    upper, lower = hi_ref[...], lo_ref[...]
    spectrum = mm(fwd_hi[...], upper) + mm(fwd_hi[...], lower) + mm(fwd_lo[...], upper)
    re, im = spectrum[: plan.modes_pad], spectrum[plan.modes_pad :]
    gr, gi = gain_re[...], gain_im[...]
    changed = jnp.concatenate([gr * re - gi * im, gr * im + gi * re], axis=0)
    upper, lower = split(changed)
    result = mm(inv_hi[...], upper) + mm(inv_hi[...], lower) + mm(inv_lo[...], upper)
    for k in range(ring):
        put_wire(plan, out_refs[k], result[k * step : k * step + lons])


def gelu_parts(pre):
    a = math.sqrt(2.0 / math.pi)
    b = a * 0.044715
    square = pre * pre
    t = jnp.tanh(pre * (a + b * square))
    half = 0.5 * pre
    hidden = half + half * t
    slope = 0.5 + 0.5 * t + half * (1.0 - t * t) * (a + 3.0 * b * square)
    return hidden, slope


def stack3(value):
    upper, lower = split(value)
    return jnp.concatenate([upper, upper, lower], axis=0)


def network_kernel(
    plan, me_ref, state_ref, sums_ref, entry3, exit3, normal3, exit_t, entry_2, *rest
):
    ring = plan.ring
    in_refs, out_refs = rest[:ring], rest[ring : 2 * ring]
    d_ref, field_ref, cells_ref = rest[2 * ring :]
    me = me_ref[0]
    rows, pitch = plan.rows, plan.pitch
    load_field(plan, field_ref, state_ref)
    add_blocks(plan, me, field_ref, in_refs)
    group = 4
    for j0 in range(0, plan.lons, group):
        js = range(j0, min(plan.lons, j0 + group))
        pieces = [field_ref[j * pitch : (j + 1) * pitch, :][:, :rows] for j in js]
        width = len(pieces) * rows
        end = min(round_up(j0 * rows + width, 128), plan.cells_pad)
        if j0 + group >= plan.lons:
            end = plan.cells_pad
        if end > j0 * rows + width:
            pieces.append(jnp.zeros((pitch, end - j0 * rows - width), F32))
        cells_ref[:, j0 * rows : end] = jnp.concatenate(pieces, axis=1)

    def one_tile(t, carry):
        at = pl.ds(pl.multiple_of(t * CELL_TILE, CELL_TILE), CELL_TILE)
        mixed = cells_ref[:, at]
        pre = mm(entry3[...], stack3(mixed))
        hidden, slope = gelu_parts(pre)
        upper, lower = split(hidden)
        both = mm(exit_t[...], upper)
        forecast = mixed + both[:pitch] + both[pitch:] + mm(exit_t[:pitch, :], lower)
        sums = sums_ref[:, at]
        count = sums[plan.variables : plan.variables + 1]
        forcing = count * mm(normal3[...], stack3(forecast)) - sums
        d_hidden = mm(exit3[...], stack3(forcing))
        upper, lower = split(d_hidden * slope)
        both = mm(entry_2[...], upper)
        cells_ref[:, at] = forcing + both[:pitch] + both[pitch:] + mm(entry_2[:pitch, :], lower)
        return carry

    lax.fori_loop(0, plan.cells_pad // CELL_TILE, one_tile, 0)
    for j in range(plan.lons):
        piece = cells_ref[:, j * rows : (j + 1) * rows]
        d_ref[j] = piece[: plan.variables]
        field_ref[j * pitch : (j + 1) * pitch, :rows] = piece
    pack_blocks(plan, me, field_ref, out_refs)


def finish_kernel(plan, me_ref, d_ref, *rest):
    in_refs, out_ref, field_ref = rest[: plan.ring], rest[plan.ring], rest[plan.ring + 1]
    load_field(plan, field_ref, d_ref)
    add_blocks(plan, me_ref[0], field_ref, in_refs)
    for j in range(plan.lons):
        row = j * plan.pitch
        out_ref[j] = field_ref[row : row + plan.variables, :][:, : plan.rows]


def observe_kernel(plan, parts, op_hi, op_lo, key_ref, seen_ref, out_ref):
    variables, pitch = plan.variables, plan.pitch
    channels = op_hi.shape[1]

    def one(d, carry):
        upper, lower = split(seen_ref[pl.ds(d, channels, stride=parts), :])
        pulled = mm(op_hi[...], upper) + mm(op_hi[...], lower) + mm(op_lo[...], upper)
        row = lax.broadcasted_iota(jnp.int32, pulled.shape, 0)
        pulled = jnp.where(row == variables, key_ref[pl.ds(d, 1), :], pulled)
        out_ref[pl.ds(pl.multiple_of(d * pitch, 8), pitch), :] = pulled
        return carry

    lax.fori_loop(0, parts, one, 0)


def collect_kernel(plan, parts, wire_ref, out_ref, total_ref):
    variables, pitch = plan.variables, plan.pitch
    group = 4
    tiles = plan.cells_pad // CELL_TILE
    total_ref[...] = jnp.zeros_like(total_ref)

    def one(g, carry):
        blocks = []
        for s in range(group):
            row = pl.multiple_of((g * group + s) * pitch, 8)
            blocks.append(wire_ref[pl.ds(row, pitch), :])
        block = jnp.concatenate(blocks, axis=1)
        key = block[variables : variables + 1].astype(jnp.int32)
        row = lax.broadcasted_iota(jnp.int32, block.shape, 0)
        upper, lower = split(jnp.where(row == variables, 1.0, block))
        value = jnp.concatenate([upper, lower], axis=0)
        low = key & (CELL_TILE - 1)
        high = key // CELL_TILE - jnp.where(key < 0, 1, 0)
        cell = lax.broadcasted_iota(jnp.int32, (CELL_TILE, block.shape[1]), 0)
        onehot = jnp.where(cell == low, 1.0, 0.0).astype(BF16)
        for t in range(tiles):
            here = jnp.where(high == t, 1.0, 0.0).astype(BF16)
            part = lax.dot_general(
                value * here, onehot, (((1,), (1,)), ((), ())), preferred_element_type=F32
            )
            total_ref[t] = total_ref[t] + part
        return carry

    lax.fori_loop(0, parts // group, one, 0)
    for t in range(tiles):
        part = total_ref[t]
        out_ref[:, t * CELL_TILE : (t + 1) * CELL_TILE] = part[:pitch] + part[pitch:]


def whole(count):
    return [pl.BlockSpec(memory_space=pltpu.VMEM)] * count


def call(kernel, name, outs, scratch, scalars, args):
    specs = [pl.BlockSpec(memory_space=pltpu.SMEM)] * len(scalars) + whole(len(args))
    many = isinstance(outs, list)
    return pl.pallas_call(
        kernel,
        out_shape=outs,
        in_specs=specs,
        out_specs=whole(len(outs)) if many else whole(1)[0],
        scratch_shapes=scratch,
        compiler_params=pltpu.CompilerParams(vmem_limit_bytes=VMEM_LIMIT),
        name=name,
    )(*scalars, *args)


def split_outside(value):
    upper = lax.reduce_precision(value, exponent_bits=8, mantissa_bits=7)
    return upper.astype(BF16), (value - upper).astype(BF16)


def make_tables(plan, me):
    step = plan.lons_pad
    column = jnp.arange(plan.ring * step, dtype=jnp.int32)
    local_lon = column % step
    lon = (me ^ (column // step)) * plan.lons + local_lon
    row = jnp.arange(2 * plan.modes_pad, dtype=jnp.int32)
    wave = row % plan.modes_pad
    is_imag = row >= plan.modes_pad
    phase = wave[:, None] * lon[None, :] % plan.nlon
    shifted = (phase + jnp.where(is_imag, plan.nlon // 4, 0)[:, None]) % plan.nlon
    table = jnp.cos(shifted.astype(F32) * (2.0 * math.pi / plan.nlon))
    live = (wave < plan.modes)[:, None] & (local_lon < plan.lons)[None, :]
    forward = jnp.where(live, table, 0.0)
    weight = jnp.where(wave == 0, 1.0, 2.0) / plan.nlon
    inverse = (forward * weight[:, None]).T
    return split_outside(forward) + split_outside(inverse)


def make_gain(plan, me, response):
    lane = jnp.arange(plan.lanes_pad, dtype=jnp.int32)
    whole_lanes = plan.full * plan.rows
    left = plan.full * plan.ring + (me * plan.left_lanes + lane - whole_lanes) // plan.rows
    variable = jnp.where(lane < whole_lanes, me * plan.full + lane // plan.rows, left)
    pick = (jnp.arange(plan.variables)[:, None] == variable[None, :]).astype(F32)
    gain = jnp.einsum("cm,cl->ml", response, pick, precision=lax.Precision.HIGHEST)
    return jnp.pad(gain, ((0, plan.modes_pad - plan.modes), (0, 0)))


def stack_rows(value):
    upper, lower = split_outside(value)
    return jnp.concatenate([upper, lower, upper], axis=1)


def stack_halves(value):
    upper, lower = split_outside(value)
    return jnp.concatenate([upper, lower], axis=0)


def exchange(blocks, ring):
    got = list(blocks)
    for k in sorted(range(1, ring), reverse=True):
        got[k] = lax.ppermute(blocks[k], "lon", [(i, i ^ k) for i in range(ring)])
    return got


def local(
    analysis_fields,
    response_inphase,
    response_quadrature,
    entry_projection_matrix,
    exit_projection_matrix,
    radiance_op,
    inv_var,
    observed,
    cell_index,
    obs_mask,
):
    ring = lax.axis_size("lon")
    variables, rows, lons = analysis_fields.shape
    plan = Plan(variables, rows, lons, ring)
    pitch = plan.pitch
    parts, slots = cell_index.shape
    lon_at = lax.axis_index("lon")
    me = lon_at.astype(jnp.int32).reshape(1)
    state = jnp.transpose(analysis_fields, (2, 0, 1))

    wire = [jax.ShapeDtypeStruct((plan.wire_rows, 128), F32)] * ring
    field = pltpu.VMEM((lons * pitch, 128), F32)
    bind = functools.partial

    blocks = call(bind(pack_kernel, plan), "pack_state", wire, [field], [me], [state])
    circles = exchange(blocks, ring)

    extra = pitch - variables
    weighted_op = jnp.pad(radiance_op * inv_var[None, :], ((0, extra), (0, 0)))
    cell = cell_index % lons * rows + cell_index // lons
    key = jnp.where(obs_mask > 0, cell, -1).astype(F32)
    seen = observed.reshape(-1, slots)
    sent = call(
        bind(observe_kernel, plan, parts),
        "pull_back",
        jax.ShapeDtypeStruct((parts * pitch, slots), F32),
        [],
        [],
        [*split_outside(weighted_op), key, seen],
    )
    arrived = lax.all_to_all(
        sent.reshape(parts, pitch, slots), ("lat", "lon"), split_axis=0, concat_axis=0, tiled=True
    ).reshape(parts * pitch, slots)

    tables = make_tables(plan, lon_at)
    gain_re = make_gain(plan, lon_at, response_inphase)
    gain_im = make_gain(plan, lon_at, response_quadrature)
    columns = pltpu.VMEM((ring * plan.lons_pad, plan.lanes_pad), BF16)

    def apply_filter(name, imag, got):
        return call(
            bind(filter_kernel, plan),
            name,
            wire,
            [columns, columns],
            [],
            [*tables, gain_re, imag, *got],
        )

    shifted = exchange(apply_filter("filter", gain_im, circles), ring)

    sums = call(
        bind(collect_kernel, plan, parts),
        "collect",
        jax.ShapeDtypeStruct((pitch, plan.cells_pad), F32),
        [pltpu.VMEM((plan.cells_pad // CELL_TILE, 2 * pitch, CELL_TILE), F32)],
        [],
        [arrived],
    )
    normal = jnp.dot(
        radiance_op * inv_var[None, :], radiance_op.T, precision=lax.Precision.HIGHEST
    )
    normal = jnp.pad(normal, ((0, extra), (0, extra)))
    entry = jnp.pad(entry_projection_matrix, ((0, extra), (0, 0)))
    leave = jnp.pad(exit_projection_matrix, ((0, 0), (0, extra)))
    out = call(
        bind(network_kernel, plan),
        "network",
        wire + [jax.ShapeDtypeStruct(state.shape, F32)],
        [field, pltpu.VMEM((pitch, plan.cells_pad), F32)],
        [me],
        [
            state,
            sums,
            stack_rows(entry.T),
            stack_rows(leave),
            stack_rows(normal),
            stack_halves(leave.T),
            stack_halves(entry),
            *shifted,
        ],
    )
    d_mixed = out[-1]
    d_circles = exchange(out[:-1], ring)
    returned = exchange(apply_filter("filter_transposed", -gain_im, d_circles), ring)
    gradient = call(
        bind(finish_kernel, plan),
        "finish",
        jax.ShapeDtypeStruct(state.shape, F32),
        [field],
        [me],
        [d_mixed, *returned],
    )
    return jnp.transpose(gradient, (1, 2, 0))


def solution(mesh):
    return jax.shard_map(
        local,
        mesh=mesh,
        in_specs=(
            P(None, "lat", "lon"),
            P(),
            P(),
            P(),
            P(),
            P(),
            P(),
            P(None, ("lat", "lon"), None),
            P(("lat", "lon"), None),
            P(("lat", "lon"), None),
        ),
        out_specs=P(None, "lat", "lon"),
        check_vma=False,
    )
```

```python
import functools
import math

import jax
import jax.numpy as jnp
from jax import lax
from jax.experimental import pallas as pl
from jax.experimental.pallas import tpu as pltpu
from jax.sharding import PartitionSpec as P

MIB = 1024 * 1024
CELL_TILE = 256
CHUNKS = 2
F32 = jnp.float32
BF16 = jnp.bfloat16


def round_up(value, unit):
    return -(-value // unit) * unit


class Plan:
    def __init__(self, variables, rows, lons, ring):
        self.variables = variables
        self.rows = rows
        self.lons = lons
        self.ring = ring
        self.pitch = round_up(variables, 8)
        self.lons_pad = round_up(lons, 16)
        self.full = variables // ring
        self.left = variables - self.full * ring
        self.left_lanes = -(-self.left * rows // ring)
        self.left_width = round_up(max(self.left_lanes * ring, 1), 128)
        self.lanes = self.full * rows + self.left_lanes
        self.lanes_pad = round_up(self.lanes, 128)
        self.tiles = self.lanes // 128
        self.rest = self.lanes - self.tiles * 128
        self.fold_width = 128
        while self.fold_width > 8 and self.fold_width // 2 >= self.rest:
            self.fold_width //= 2
        self.folds = 128 // self.fold_width
        self.tail = -(-lons // self.folds) if self.rest else 0
        self.starts = [min(i * self.tail, lons - self.tail) for i in range(self.folds)]
        self.wire_rows = round_up(self.tiles * lons + self.tail, 8)
        self.cells = lons * rows
        self.cells_pad = round_up(self.cells, CELL_TILE)
        self.nlon = lons * ring
        self.modes = self.nlon // 2
        self.modes_pad = round_up(self.modes, 8)


def split(value):
    upper = value.astype(BF16)
    lower = (value - upper.astype(F32)).astype(BF16)
    return upper, lower


def mm(a, b):
    return jnp.dot(a, b, preferred_element_type=F32)


def put_wire(plan, place, block):
    ref, base = place
    lons = plan.lons
    for t in range(plan.tiles):
        row = base + t * lons
        ref[row : row + lons, :] = block[:, t * 128 : (t + 1) * 128]
    if plan.rest == 0:
        return
    last = block[:, plan.tiles * 128 :]
    pieces = [last[at : at + plan.tail, : plan.fold_width] for at in plan.starts]
    row = base + plan.tiles * lons
    ref[row : row + plan.tail, :] = jnp.concatenate(pieces, axis=1)


def get_wire(plan, place):
    ref, base = place
    lons = plan.lons
    found = []
    for t in range(plan.tiles):
        row = base + t * lons
        found.append(ref[row : row + lons, :])
    if plan.rest > 0:
        row = base + plan.tiles * lons
        last = ref[row : row + plan.tail, :]
        pieces = []
        for i, at in enumerate(plan.starts):
            turned = last if i == 0 else pltpu.roll(last, 128 - i * plan.fold_width, 1)
            pieces.append(turned[i * plan.tail - at :])
        found.append(jnp.concatenate(pieces, axis=0) if len(pieces) > 1 else pieces[0])
    return found


def sent_places(plan, refs, chunks=1, chunk=0):
    rows = plan.wire_rows
    return [(refs[k // 2], (k % 2 * chunks + chunk) * rows) for k in range(plan.ring)]


def got_places(plan, refs, chunks=1, chunk=0):
    rows, chips = plan.wire_rows, plan.ring // 2
    return [
        (refs[k % 2 * chips + k // 2], (k % 2 * chunks + chunk) * rows) for k in range(plan.ring)
    ]


def pack_blocks(plan, me, field_ref, places):
    lons, rows = plan.lons, plan.rows

    def variable(c):
        return field_ref[pl.ds(c, lons, stride=plan.pitch), :][:, :rows]

    left = None
    if plan.left > 0:
        first = plan.full * plan.ring
        pieces = [variable(first + i) for i in range(plan.left)]
        spare = plan.left_width - plan.left * rows
        if spare > 0:
            pieces.append(jnp.zeros((lons, spare), F32))
        left = jnp.concatenate(pieces, axis=1)
    for k, place in enumerate(places):
        q = me ^ k
        pieces = [variable(q * plan.full + i) for i in range(plan.full)]
        if left is not None:
            shift = lax.rem(plan.left_width - q * plan.left_lanes, plan.left_width)
            pieces.append(pltpu.roll(left, shift, 1)[:, : plan.left_lanes])
        spare = plan.lanes_pad - plan.lanes
        if spare > 0:
            pieces.append(jnp.zeros((lons, spare), F32))
        put_wire(plan, place, jnp.concatenate(pieces, axis=1))


def add_blocks(plan, me, field_ref, places):
    lons, rows = plan.lons, plan.rows
    left = jnp.zeros((lons, plan.left_width), F32)
    lane = lax.broadcasted_iota(jnp.int32, (lons, plan.left_width), 1)
    for k, place in enumerate(places):
        q = me ^ k
        block = jnp.concatenate(get_wire(plan, place), axis=1)
        for i in range(plan.full):
            at = pl.ds(q * plan.full + i, lons, stride=plan.pitch)
            piece = block[:, i * rows : (i + 1) * rows]
            field_ref[at, :] = field_ref[at, :] + jnp.pad(piece, ((0, 0), (0, 128 - rows)))
        if plan.left > 0:
            piece = block[:, plan.full * rows : plan.lanes]
            piece = jnp.pad(piece, ((0, 0), (0, plan.left_width - plan.left_lanes)))
            left = left + pltpu.roll(piece, q * plan.left_lanes, 1)
    for i in range(plan.left):
        at = pl.ds(plan.full * plan.ring + i, lons, stride=plan.pitch)
        piece = left[:, i * rows : (i + 1) * rows]
        field_ref[at, :] = field_ref[at, :] + jnp.pad(piece, ((0, 0), (0, 128 - rows)))


def load_field(plan, field_ref, source_ref, first):
    pad = jnp.zeros((plan.pitch, 128), F32)
    for j in range(plan.lons):
        row = j * plan.pitch
        field_ref[row : row + plan.pitch, :] = pad
        piece = source_ref[j][:, first : first + plan.rows]
        field_ref[row : row + plan.variables, : plan.rows] = piece


def pack_kernel(plan, chunks, me_ref, state_ref, *rest):
    out_refs, field_ref = rest[:-1], rest[-1]
    for h in range(chunks):
        load_field(plan, field_ref, state_ref, h * plan.rows)
        places = sent_places(plan, out_refs, chunks, h)
        pack_blocks(plan, me_ref[0], field_ref, places)


def filter_kernel(plan, chunks, fwd_hi, fwd_lo, inv_hi, inv_lo, gain_re, gain_im, *rest):
    ring = plan.ring
    chips = ring // 2
    in_refs, rest = rest[:ring], rest[ring:]
    out_refs, (hi_ref, lo_ref) = rest[: chunks * chips], rest[chunks * chips :]
    lons, step, width = plan.lons, plan.lons_pad, plan.lanes_pad
    for h in range(chunks):
        for k, place in enumerate(got_places(plan, in_refs, chunks, h)):
            for t, tile in enumerate(get_wire(plan, place)):
                tile = jnp.concatenate([tile, jnp.zeros((step - lons, 128), F32)], axis=0)
                upper, lower = split(tile)
                at = h * width + t * 128
                hi_ref[k * step : (k + 1) * step, at : at + 128] = upper
                lo_ref[k * step : (k + 1) * step, at : at + 128] = lower
    gr, gi = gain_re[...], gain_im[...]
    for h in range(chunks):
        upper = hi_ref[:, h * width : (h + 1) * width]
        lower = lo_ref[:, h * width : (h + 1) * width]
        spectrum = mm(fwd_hi[...], upper) + mm(fwd_hi[...], lower) + mm(fwd_lo[...], upper)
        re, im = spectrum[: plan.modes_pad], spectrum[plan.modes_pad :]
        changed = jnp.concatenate([gr * re - gi * im, gr * im + gi * re], axis=0)
        upper, lower = split(changed)
        result = mm(inv_hi[...], upper) + mm(inv_hi[...], lower) + mm(inv_lo[...], upper)
        places = sent_places(plan, out_refs[h * chips : (h + 1) * chips])
        for k, place in enumerate(places):
            put_wire(plan, place, result[k * step : k * step + lons])


def gelu_parts(pre):
    a = math.sqrt(2.0 / math.pi)
    b = a * 0.044715
    square = pre * pre
    s = 0.5 + 0.5 * jnp.tanh(pre * (a + b * square))
    hidden = pre * s
    slope = s * (1.0 + pre * (2.0 * a + 6.0 * b * square) * (1.0 - s))
    return hidden, slope


def stack3(value):
    upper, lower = split(value)
    return jnp.concatenate([upper, upper, lower], axis=0)


def network_kernel(
    plan, first, me_ref, state_ref, sums_ref, entry3, exit3, normal3, exit_t, entry_2, *rest
):
    ring = plan.ring
    count = ring + ring // 2
    sources = got_places(plan, rest[:ring])
    targets = sent_places(plan, rest[ring:count])
    d_ref, field_ref, cells_ref = rest[count:]
    start = first // plan.rows * plan.cells_pad
    me = me_ref[0]
    rows, pitch = plan.rows, plan.pitch
    load_field(plan, field_ref, state_ref, first)
    add_blocks(plan, me, field_ref, sources)
    group = 8
    for j0 in range(0, plan.lons, group):
        js = range(j0, min(plan.lons, j0 + group))
        pieces = [field_ref[j * pitch : (j + 1) * pitch, :][:, :rows] for j in js]
        width = len(pieces) * rows
        end = min(round_up(j0 * rows + width, 128), plan.cells_pad)
        if j0 + group >= plan.lons:
            end = plan.cells_pad
        if end > j0 * rows + width:
            pieces.append(jnp.zeros((pitch, end - j0 * rows - width), F32))
        cells_ref[:, j0 * rows : end] = jnp.concatenate(pieces, axis=1)

    def one_tile(t, carry):
        at = pl.ds(pl.multiple_of(t * CELL_TILE, CELL_TILE), CELL_TILE)
        mixed = cells_ref[:, at]
        pre = mm(entry3[...], stack3(mixed))
        hidden, slope = gelu_parts(pre)
        upper, lower = split(hidden)
        both = mm(exit_t[...], upper)
        forecast = mixed + both[:pitch] + both[pitch:] + mm(exit_t[:pitch, :], lower)
        there = pl.multiple_of(start + t * CELL_TILE, CELL_TILE)
        sums = sums_ref[:, pl.ds(there, CELL_TILE)]
        count = sums[plan.variables : plan.variables + 1]
        forcing = count * mm(normal3[...], stack3(forecast)) - sums
        d_hidden = mm(exit3[...], stack3(forcing))
        upper, lower = split(d_hidden * slope)
        both = mm(entry_2[...], upper)
        cells_ref[:, at] = forcing + both[:pitch] + both[pitch:] + mm(entry_2[:pitch, :], lower)
        return carry

    lax.fori_loop(0, plan.cells_pad // CELL_TILE, one_tile, 0)
    for j in range(plan.lons):
        piece = cells_ref[:, j * rows : (j + 1) * rows]
        d_ref[j] = piece[: plan.variables]
        field_ref[j * pitch : (j + 1) * pitch, :rows] = piece
    pack_blocks(plan, me, field_ref, targets)


def finish_kernel(plan, chunks, me_ref, *rest):
    d_refs, rest = rest[:chunks], rest[chunks:]
    count = plan.ring
    out_ref, field_refs = rest[chunks * count], rest[chunks * count + 1 :]
    for h in range(chunks):
        load_field(plan, field_refs[h], d_refs[h], 0)
        places = got_places(plan, rest[h * count : (h + 1) * count])
        add_blocks(plan, me_ref[0], field_refs[h], places)
    for j in range(plan.lons):
        row = j * plan.pitch
        pieces = [ref[row : row + plan.variables, :][:, : plan.rows] for ref in field_refs]
        out_ref[j] = jnp.concatenate(pieces, axis=1)


def observe_kernel(plan, parts, op_hi, op_lo, key_ref, seen_ref, out_ref):
    variables, pitch = plan.variables, plan.pitch
    channels = op_hi.shape[1]

    def one(d, carry):
        upper, lower = split(seen_ref[pl.ds(d, channels, stride=parts), :])
        pulled = mm(op_hi[...], upper) + mm(op_hi[...], lower) + mm(op_lo[...], upper)
        row = lax.broadcasted_iota(jnp.int32, pulled.shape, 0)
        pulled = jnp.where(row == variables, key_ref[pl.ds(d, 1), :], pulled)
        out_ref[pl.ds(pl.multiple_of(d * pitch, 8), pitch), :] = pulled
        return carry

    lax.fori_loop(0, parts, one, 0)


def collect_kernel(plan, chunks, parts, wire_ref, out_ref, masked_ref, total_ref):
    variables, pitch = plan.variables, plan.pitch
    tiles = chunks * plan.cells_pad // CELL_TILE
    slots = wire_ref.shape[1]
    group = masked_ref.shape[1] // slots
    total_ref[...] = jnp.zeros_like(total_ref)

    def one(g, carry):
        blocks = []
        for s in range(group):
            row = pl.multiple_of((g * group + s) * pitch, 8)
            blocks.append(wire_ref[pl.ds(row, pitch), :])
        block = jnp.concatenate(blocks, axis=1)
        key = block[variables : variables + 1].astype(jnp.int32)
        row = lax.broadcasted_iota(jnp.int32, block.shape, 0)
        upper, lower = split(jnp.where(row == variables, 1.0, block))
        value = jnp.concatenate([upper, lower], axis=0)
        low = key & (CELL_TILE - 1)
        high = key // CELL_TILE - jnp.where(key < 0, 1, 0)
        cell = lax.broadcasted_iota(jnp.int32, (CELL_TILE, block.shape[1]), 0)
        onehot = jnp.where(cell == low, 1.0, 0.0).astype(BF16)
        for t in range(tiles):
            here = jnp.where(high == t, 1.0, 0.0).astype(BF16)
            masked_ref[t * 2 * pitch : (t + 1) * 2 * pitch, :] = value * here
        total_ref[...] = total_ref[...] + lax.dot_general(
            masked_ref[...], onehot, (((1,), (1,)), ((), ())), preferred_element_type=F32
        )
        return carry

    lax.fori_loop(0, parts // group, one, 0)
    for t in range(tiles):
        row = t * 2 * pitch
        out_ref[:, t * CELL_TILE : (t + 1) * CELL_TILE] = (
            total_ref[row : row + pitch] + total_ref[row + pitch : row + 2 * pitch]
        )


def whole(count):
    return [pl.BlockSpec(memory_space=pltpu.VMEM)] * count


def call(kernel, name, outs, scratch, scalars, args, microseconds):
    specs = [pl.BlockSpec(memory_space=pltpu.SMEM)] * len(scalars) + whole(len(args))
    many = isinstance(outs, list)
    return pl.pallas_call(
        kernel,
        out_shape=outs,
        in_specs=specs,
        out_specs=whole(len(outs)) if many else whole(1)[0],
        scratch_shapes=scratch,
        compiler_params=pltpu.CompilerParams(vmem_limit_bytes=(56 if lax.axis_size("lon") > 8 else 24) * MIB),
        cost_estimate=pl.CostEstimate(
            flops=microseconds * 1_000_000_000, bytes_accessed=1_000_000, transcendentals=0
        ),
        name=name,
    )(*scalars, *args)


def split_outside(value):
    upper = lax.reduce_precision(value, exponent_bits=8, mantissa_bits=7)
    return upper.astype(BF16), (value - upper).astype(BF16)


def make_tables(plan, me):
    step = plan.lons_pad
    column = jnp.arange(plan.ring * step, dtype=jnp.int32)
    local_lon = column % step
    lon = (me ^ (column // step)) * plan.lons + local_lon
    row = jnp.arange(2 * plan.modes_pad, dtype=jnp.int32)
    wave = row % plan.modes_pad
    quarter = jnp.where(row >= plan.modes_pad, 0.5 * math.pi, 0.0).astype(F32)
    phase = wave[:, None] * lon[None, :] % plan.nlon
    table = jnp.cos(phase.astype(F32) * (2.0 * math.pi / plan.nlon) + quarter[:, None])
    live = (wave < plan.modes)[:, None] & (local_lon < plan.lons)[None, :]
    forward = lax.optimization_barrier(split_outside(jnp.where(live, table, 0.0)))
    return forward + (forward[0].T, forward[1].T)


def make_gain(plan, me, response):
    lane = jnp.arange(plan.lanes_pad, dtype=jnp.int32)
    whole_lanes = plan.full * plan.rows
    left = plan.full * plan.ring + (me * plan.left_lanes + lane - whole_lanes) // plan.rows
    variable = jnp.where(lane < whole_lanes, me * plan.full + lane // plan.rows, left)
    pick = (jnp.arange(plan.variables)[:, None] == variable[None, :]).astype(F32)
    gain = jnp.einsum("cm,cl->ml", response, pick, precision=lax.Precision.HIGHEST)
    weight = jnp.where(jnp.arange(plan.modes) == 0, 1.0, 2.0) / plan.nlon
    gain = gain * weight[:, None]
    return jnp.pad(gain, ((0, plan.modes_pad - plan.modes), (0, 0)))


def stack_rows(value):
    upper, lower = split_outside(value)
    return jnp.concatenate([upper, lower, upper], axis=1)


def stack_halves(value):
    upper, lower = split_outside(value)
    return jnp.concatenate([upper, lower], axis=0)


def between_chips(pairs, ring):
    got = list(pairs)
    for k in sorted(range(1, ring // 2), reverse=True):
        got[k] = lax.ppermute(pairs[k], "lon", [(i, i ^ (2 * k)) for i in range(ring)])
    return got


def between_cores(got, ring):
    swap = [(i, i ^ 1) for i in range(ring)]
    return [*got, *(lax.ppermute(pair, "lon", swap) for pair in got)]


def after(values, *others):
    return lax.optimization_barrier((values, others))[0]


def local(
    analysis_fields,
    response_inphase,
    response_quadrature,
    entry_projection_matrix,
    exit_projection_matrix,
    radiance_op,
    inv_var,
    observed,
    cell_index,
    obs_mask,
):
    ring = lax.axis_size("lon")
    variables, rows, lons = analysis_fields.shape
    chunks = CHUNKS
    plan = Plan(variables, rows // chunks, lons, ring)
    chips = ring // 2
    pitch = plan.pitch
    parts, slots = cell_index.shape
    lon_at = lax.axis_index("lon")
    me = lon_at.astype(jnp.int32).reshape(1)
    state = jnp.transpose(analysis_fields, (2, 0, 1))

    def wire(count):
        return [jax.ShapeDtypeStruct((2 * count * plan.wire_rows, 128), F32)] * chips

    field = pltpu.VMEM((lons * pitch, 128), F32)
    bind = functools.partial

    blocks = call(
        bind(pack_kernel, plan, chunks), "pack_state", wire(chunks), [field], [me], [state], 4
    )
    circles = between_chips(blocks, ring)

    extra = pitch - variables
    weighted_op = radiance_op * inv_var[None, :]
    padded_op = after(jnp.pad(weighted_op, ((0, extra), (0, 0))), blocks[0])
    row, lon = cell_index // lons, cell_index % lons
    cell = row // plan.rows * plan.cells_pad + lon * plan.rows + row % plan.rows
    key = jnp.where(obs_mask > 0, cell, -1).astype(F32)
    sent = call(
        bind(observe_kernel, plan, parts),
        "pull_back",
        jax.ShapeDtypeStruct((parts * pitch, slots), F32),
        [],
        [],
        [*split_outside(padded_op), key, observed.reshape(-1, slots)],
        13,
    )
    arrived = lax.all_to_all(
        sent.reshape(parts, pitch, slots), ("lat", "lon"), split_axis=0, concat_axis=0, tiled=True
    ).reshape(parts * pitch, slots)

    tables = make_tables(plan, lon_at)
    gain_re = make_gain(plan, lon_at, response_inphase)
    gain_im = make_gain(plan, lon_at, response_quadrature)

    def apply_filter(name, imag, got, count):
        columns = pltpu.VMEM((ring * plan.lons_pad, count * plan.lanes_pad), BF16)
        out = call(
            bind(filter_kernel, plan, count),
            name,
            wire(1) * count,
            [columns, columns],
            [],
            [*tables, gain_re, imag, *got],
            4 * count,
        )
        return [out[h * chips : (h + 1) * chips] for h in range(count)]

    circles = between_cores(after(circles, sent, tables, gain_re, gain_im), ring)
    shifted = apply_filter("filter", gain_im, circles, chunks)
    shifted = [between_chips(pairs, ring) for pairs in shifted]

    normal = jnp.dot(weighted_op, radiance_op.T, precision=lax.Precision.HIGHEST)
    normal = jnp.pad(normal, ((0, extra), (0, extra)))
    entry = jnp.pad(entry_projection_matrix, ((0, extra), (0, 0)))
    leave = jnp.pad(exit_projection_matrix, ((0, 0), (0, extra)))
    weights = [
        stack_rows(entry.T),
        stack_rows(leave),
        stack_rows(normal),
        stack_halves(leave.T),
        stack_halves(entry),
    ]
    total_rows = chunks * plan.cells_pad // CELL_TILE * 2 * pitch
    sums = call(
        bind(collect_kernel, plan, chunks, parts),
        "collect",
        jax.ShapeDtypeStruct((pitch, chunks * plan.cells_pad), F32),
        [
            pltpu.VMEM((total_rows, 8 * slots), BF16),
            pltpu.VMEM((total_rows, CELL_TILE), F32),
        ],
        [],
        [after(arrived, weights)],
        8,
    )
    waits = sums
    d_mixed, d_circles = [], []
    for h in range(chunks):
        got = between_cores(after(shifted[h], waits), ring)
        out = call(
            bind(network_kernel, plan, h * plan.rows),
            "network",
            wire(1) + [jax.ShapeDtypeStruct((lons, variables, plan.rows), F32)],
            [field, pltpu.VMEM((pitch, plan.cells_pad), F32)],
            [me],
            [state, sums, *weights, *got],
            16,
        )
        waits = out[0]
        d_mixed.append(out[-1])
        d_circles.append(between_chips(out[:-1], ring))
    returned = []
    for h in range(chunks):
        got = between_cores(after(d_circles[h], waits), ring)
        out = apply_filter("filter_transposed", -gain_im, got, 1)[0]
        waits = out[0]
        returned.append(between_chips(out, ring))
    arrivals = []
    for h in range(chunks):
        arrivals += between_cores(after(returned[h], waits), ring)
    gradient = call(
        bind(finish_kernel, plan, chunks),
        "finish",
        jax.ShapeDtypeStruct(state.shape, F32),
        [field] * chunks,
        [me],
        [*d_mixed, *arrivals],
        4,
    )
    return jnp.transpose(gradient, (1, 2, 0))


def solution(mesh):
    return jax.shard_map(
        local,
        mesh=mesh,
        in_specs=(
            P(None, "lat", "lon"),
            P(),
            P(),
            P(),
            P(),
            P(),
            P(),
            P(None, ("lat", "lon"), None),
            P(("lat", "lon"), None),
            P(("lat", "lon"), None),
        ),
        out_specs=P(None, "lat", "lon"),
        check_vma=False,
    )
```

```python
import functools
import math

import jax
import jax.numpy as jnp
from jax import lax
from jax.experimental import pallas as pl
from jax.experimental.pallas import tpu as pltpu
from jax.sharding import PartitionSpec as P

MIB = 1024 * 1024
CELL_TILE = 256
CHUNKS = 2
SHORT, W1, W2, LONG = 0, 10_000, 6_000, 50_000
F32 = jnp.float32
BF16 = jnp.bfloat16


def round_up(value, unit):
    return -(-value // unit) * unit


class Plan:
    def __init__(self, variables, rows, lons, ring):
        self.variables = variables
        self.rows = rows
        self.lons = lons
        self.ring = ring
        self.pitch = round_up(variables, 8)
        self.lons_pad = round_up(lons, 16)
        self.full = variables // ring
        self.left = variables - self.full * ring
        self.left_lanes = -(-self.left * rows // ring)
        self.left_width = round_up(max(self.left_lanes * ring, 1), 128)
        self.lanes = self.full * rows + self.left_lanes
        self.lanes_pad = round_up(self.lanes, 128)
        self.tiles = self.lanes // 128
        self.rest = self.lanes - self.tiles * 128
        self.fold_width = 128
        while self.fold_width > 8 and self.fold_width // 2 >= self.rest:
            self.fold_width //= 2
        self.folds = 128 // self.fold_width
        self.tail = -(-lons // self.folds) if self.rest else 0
        self.starts = [min(i * self.tail, lons - self.tail) for i in range(self.folds)]
        self.wire_rows = self.tiles * lons + self.tail
        self.cells = lons * rows
        self.cells_pad = round_up(self.cells, 128)
        self.nlon = lons * ring
        self.modes = self.nlon // 2
        self.modes_pad = round_up(self.modes, 8)


def split(value):
    upper = value.astype(BF16)
    lower = (value - upper.astype(F32)).astype(BF16)
    return upper, lower


def mm(a, b):
    return jnp.dot(a, b, preferred_element_type=F32)


def put_wire(plan, place, block):
    ref, base = place
    lons = plan.lons
    for t in range(plan.tiles):
        row = base + t * lons
        ref[row : row + lons, :] = block[:, t * 128 : (t + 1) * 128]
    if plan.rest == 0:
        return
    last = block[:, plan.tiles * 128 :]
    pieces = [last[at : at + plan.tail, : plan.fold_width] for at in plan.starts]
    row = base + plan.tiles * lons
    ref[row : row + plan.tail, :] = jnp.concatenate(pieces, axis=1)


def get_wire(plan, place):
    ref, base = place
    lons = plan.lons
    found = []
    for t in range(plan.tiles):
        row = base + t * lons
        found.append(ref[row : row + lons, :])
    if plan.rest > 0:
        row = base + plan.tiles * lons
        last = ref[row : row + plan.tail, :]
        pieces = []
        for i, at in enumerate(plan.starts):
            turned = last if i == 0 else pltpu.roll(last, 128 - i * plan.fold_width, 1)
            pieces.append(turned[i * plan.tail - at :])
        found.append(jnp.concatenate(pieces, axis=0) if len(pieces) > 1 else pieces[0])
    return found


def sent_places(plan, refs, chunks=1, chunk=0):
    rows = plan.wire_rows
    places = [(refs[k // 2], (k % 2 * chunks + chunk) * rows) for k in range(plan.ring)]
    return places, refs[plan.ring // 2 :]


def got_places(plan, refs, chunks=1, chunk=0):
    rows, chips = plan.wire_rows, plan.ring // 2
    places = [
        (refs[k % 2 * chips + k // 2], (k % 2 * chunks + chunk) * rows) for k in range(plan.ring)
    ]
    return places, refs[plan.ring :]


def pack_blocks(plan, me, field_ref, places):
    lons, rows = plan.lons, plan.rows

    def variable(c):
        return field_ref[pl.ds(c, lons, stride=plan.pitch), :][:, :rows]

    left = None
    if plan.left > 0:
        first = plan.full * plan.ring
        pieces = [variable(first + i) for i in range(plan.left)]
        spare = plan.left_width - plan.left * rows
        if spare > 0:
            pieces.append(jnp.zeros((lons, spare), F32))
        left = jnp.concatenate(pieces, axis=1)
    for k, place in enumerate(places):
        q = me ^ k
        pieces = [variable(q * plan.full + i) for i in range(plan.full)]
        if left is not None:
            shift = lax.rem(plan.left_width - q * plan.left_lanes, plan.left_width)
            pieces.append(pltpu.roll(left, shift, 1)[:, : plan.left_lanes])
        spare = plan.lanes_pad - plan.lanes
        if spare > 0:
            pieces.append(jnp.zeros((lons, spare), F32))
        put_wire(plan, place, jnp.concatenate(pieces, axis=1))


def add_blocks(plan, me, field_ref, places):
    lons, rows = plan.lons, plan.rows
    left = jnp.zeros((lons, plan.left_width), F32)
    lane = lax.broadcasted_iota(jnp.int32, (lons, plan.left_width), 1)
    for k, place in enumerate(places):
        q = me ^ k
        block = jnp.concatenate(get_wire(plan, place), axis=1)
        for i in range(plan.full):
            at = pl.ds(q * plan.full + i, lons, stride=plan.pitch)
            piece = block[:, i * rows : (i + 1) * rows]
            field_ref[at, :] = field_ref[at, :] + jnp.pad(piece, ((0, 0), (0, 128 - rows)))
        if plan.left > 0:
            piece = block[:, plan.full * rows : plan.lanes]
            piece = jnp.pad(piece, ((0, 0), (0, plan.left_width - plan.left_lanes)))
            left = left + pltpu.roll(piece, q * plan.left_lanes, 1)
    for i in range(plan.left):
        at = pl.ds(plan.full * plan.ring + i, lons, stride=plan.pitch)
        piece = left[:, i * rows : (i + 1) * rows]
        field_ref[at, :] = field_ref[at, :] + jnp.pad(piece, ((0, 0), (0, 128 - rows)))


def load_field(plan, field_ref, source_ref, first):
    pad = jnp.zeros((plan.pitch, 128), F32)
    for j in range(plan.lons):
        row = j * plan.pitch
        field_ref[row : row + plan.pitch, :] = pad
        piece = source_ref[j][:, first : first + plan.rows]
        field_ref[row : row + plan.variables, : plan.rows] = piece


def pack_kernel(plan, chunks, me_ref, state_ref, *rest):
    out_refs, field_ref = rest[:-1], rest[-1]
    me = me_ref[0]
    for h in range(chunks):
        load_field(plan, field_ref, state_ref, h * plan.rows)
        places, _ = sent_places(plan, out_refs, chunks, h)
        pack_blocks(plan, me, field_ref, places)


def filter_kernel(
    plan, chunks, fwd_hi, fwd_lo, inv_hi, inv_lo, gain_re, gain_im, *rest
):
    refs, sources, targets = rest, [], []
    for h in range(chunks):
        places, rest = got_places(plan, refs, chunks, h)
        sources.append(places)
    for _ in range(chunks):
        places, rest = sent_places(plan, rest)
        targets.append(places)
    hi_ref, lo_ref = rest
    lons, step, width = plan.lons, plan.lons_pad, plan.lanes_pad
    for h in range(chunks):
        for k, place in enumerate(sources[h]):
            for t, tile in enumerate(get_wire(plan, place)):
                tile = jnp.concatenate([tile, jnp.zeros((step - lons, 128), F32)], axis=0)
                upper, lower = split(tile)
                at = h * width + t * 128
                hi_ref[k * step : (k + 1) * step, at : at + 128] = upper
                lo_ref[k * step : (k + 1) * step, at : at + 128] = lower
    gr, gi = gain_re[...], gain_im[...]
    for h in range(chunks):
        upper = hi_ref[:, h * width : (h + 1) * width]
        lower = lo_ref[:, h * width : (h + 1) * width]
        spectrum = mm(fwd_hi[...], upper) + mm(fwd_hi[...], lower) + mm(fwd_lo[...], upper)
        re, im = spectrum[: plan.modes_pad], spectrum[plan.modes_pad :]
        changed = jnp.concatenate([gr * re - gi * im, gr * im + gi * re], axis=0)
        upper, lower = split(changed)
        result = mm(inv_hi[...], upper) + mm(inv_hi[...], lower) + mm(inv_lo[...], upper)
        for k, place in enumerate(targets[h]):
            put_wire(plan, place, result[k * step : k * step + lons])


def gelu_parts(pre):
    a = math.sqrt(2.0 / math.pi)
    b = a * 0.044715
    square = pre * pre
    s = 0.5 + 0.5 * jnp.tanh(pre * (a + b * square))
    hidden = pre * s
    slope = s * (1.0 + pre * (2.0 * a + 6.0 * b * square) * (1.0 - s))
    return hidden, slope


def stack3(value):
    upper, lower = split(value)
    return jnp.concatenate([upper, upper, lower], axis=0)


def each_tile(count, one_tile):
    def step(t, carry):
        one_tile(pl.multiple_of(t * CELL_TILE, CELL_TILE), CELL_TILE)
        return carry

    tiles = count // CELL_TILE
    lax.fori_loop(0, tiles, step, 0)
    if count > tiles * CELL_TILE:
        one_tile(tiles * CELL_TILE, count - tiles * CELL_TILE)


def product2(stacked, value, pitch):
    upper, lower = split(value)
    both = mm(stacked[...], upper)
    return both[:pitch] + both[pitch:] + mm(stacked[:pitch, :], lower)


def network_kernel(
    plan, chunk, me_ref, state_ref, sums_ref, entry3, exit3, normal3, exit_2, entry_2, *rest
):
    me = me_ref[0]
    sources, rest = got_places(plan, rest)
    targets, (d_ref, field_ref, cells_ref) = sent_places(plan, rest)
    rows, pitch = plan.rows, plan.pitch
    start = chunk * plan.cells_pad
    load_field(plan, field_ref, state_ref, chunk * rows)
    add_blocks(plan, me, field_ref, sources)
    group = 8
    for j0 in range(0, plan.lons, group):
        js = range(j0, min(plan.lons, j0 + group))
        pieces = [field_ref[j * pitch : (j + 1) * pitch, :][:, :rows] for j in js]
        end = min(round_up((j0 + len(pieces)) * rows, 128), plan.cells_pad)
        spare = end - (j0 + len(pieces)) * rows
        if spare > 0:
            pieces.append(jnp.zeros((pitch, spare), F32))
        cells_ref[:, j0 * rows : end] = jnp.concatenate(pieces, axis=1)

    def one_tile(first, width):
        at = pl.ds(first, width)
        mixed = cells_ref[:, at]
        hidden, slope = gelu_parts(mm(entry3[...], stack3(mixed)))
        forecast = mixed + product2(exit_2, hidden, pitch)
        sums = sums_ref[:, pl.ds(pl.multiple_of(start + first, 128), width)]
        count = sums[plan.variables : plan.variables + 1]
        forcing = count * mm(normal3[...], stack3(forecast)) - sums
        d_hidden = mm(exit3[...], stack3(forcing))
        cells_ref[:, at] = forcing + product2(entry_2, d_hidden * slope, pitch)

    each_tile(plan.cells_pad, one_tile)
    for j in range(plan.lons):
        piece = cells_ref[:, j * rows : (j + 1) * rows]
        d_ref[j] = piece[: plan.variables]
        field_ref[j * pitch : (j + 1) * pitch, :rows] = piece
    pack_blocks(plan, me, field_ref, targets)


def finish_kernel(plan, chunks, me_ref, *rest):
    me = me_ref[0]
    d_refs, rest = rest[:chunks], rest[chunks:]
    sources = []
    for h in range(chunks):
        places, rest = got_places(plan, rest)
        sources.append(places)
    out_ref, field_refs = rest[0], rest[1:]
    for h in range(chunks):
        load_field(plan, field_refs[h], d_refs[h], 0)
        add_blocks(plan, me, field_refs[h], sources[h])
    for j in range(plan.lons):
        row = j * plan.pitch
        pieces = [ref[row : row + plan.variables, :][:, : plan.rows] for ref in field_refs]
        out_ref[j] = jnp.concatenate(pieces, axis=1)


def observe_kernel(plan, parts, op_hi, op_lo, key_ref, seen_ref, out_ref):
    variables, pitch = plan.variables, plan.pitch
    channels = op_hi.shape[1]

    def one(d, carry):
        upper, lower = split(seen_ref[pl.ds(d, channels, stride=parts), :])
        pulled = mm(op_hi[...], upper) + mm(op_hi[...], lower) + mm(op_lo[...], upper)
        row = lax.broadcasted_iota(jnp.int32, pulled.shape, 0)
        pulled = jnp.where(row == variables, key_ref[pl.ds(d, 1), :], pulled)
        out_ref[pl.ds(pl.multiple_of(d * pitch, 8), pitch), :] = pulled
        return carry

    lax.fori_loop(0, parts, one, 0)


def collect_kernel(plan, chunks, parts, wire_ref, out_ref, masked_ref, total_ref):
    variables, pitch = plan.variables, plan.pitch
    tiles = -(-chunks * plan.cells_pad // CELL_TILE)
    slots = wire_ref.shape[1]
    group = masked_ref.shape[1] // slots
    total_ref[...] = jnp.zeros_like(total_ref)

    def one(g, carry):
        blocks = []
        for s in range(group):
            row = pl.multiple_of((g * group + s) * pitch, 8)
            blocks.append(wire_ref[pl.ds(row, pitch), :])
        block = jnp.concatenate(blocks, axis=1)
        key = block[variables : variables + 1].astype(jnp.int32)
        row = lax.broadcasted_iota(jnp.int32, block.shape, 0)
        upper, lower = split(jnp.where(row == variables, 1.0, block))
        value = jnp.concatenate([upper, lower], axis=0)
        low = key & (CELL_TILE - 1)
        high = key // CELL_TILE - jnp.where(key < 0, 1, 0)
        cell = lax.broadcasted_iota(jnp.int32, (CELL_TILE, block.shape[1]), 0)
        onehot = jnp.where(cell == low, 1.0, 0.0).astype(BF16)
        for t in range(tiles):
            here = jnp.where(high == t, 1.0, 0.0).astype(BF16)
            masked_ref[t * 2 * pitch : (t + 1) * 2 * pitch, :] = value * here
        total_ref[...] = total_ref[...] + lax.dot_general(
            masked_ref[...], onehot, (((1,), (1,)), ((), ())), preferred_element_type=F32
        )
        return carry

    lax.fori_loop(0, parts // group, one, 0)
    for t in range(tiles):
        row = t * 2 * pitch
        part = total_ref[row : row + pitch] + total_ref[row + pitch : row + 2 * pitch]
        width = min(CELL_TILE, out_ref.shape[1] - t * CELL_TILE)
        out_ref[:, t * CELL_TILE : t * CELL_TILE + width] = part[:, :width]


def weights_kernel(plan, entry_ref, leave_ref, op_ref, var_ref, *outs):
    entry3, leave3, normal3, leave_2, entry_2, op_hi, op_lo = outs
    extra = plan.pitch - plan.variables

    def padded(ref):
        value = ref[...]
        return jnp.concatenate([value, jnp.zeros((extra, value.shape[1]), F32)], axis=0)

    for ref, out3, out2 in ((entry_ref, entry3, entry_2), (leave_ref, leave3, leave_2)):
        value = padded(ref)
        upper, lower = split(value)
        out2[...] = jnp.concatenate([upper, lower], axis=0)
        upper, lower = split(value.T)
        out3[...] = jnp.concatenate([upper, lower, upper], axis=1)
    op = padded(op_ref)
    weighted = op * var_ref[...]
    upper, lower = split(weighted)
    op_hi[...] = upper
    op_lo[...] = lower
    normal = lax.dot_general(
        weighted,
        op,
        (((1,), (1,)), ((), ())),
        precision=lax.Precision.HIGHEST,
        preferred_element_type=F32,
    )
    upper, lower = split(normal)
    normal3[...] = jnp.concatenate([upper, lower, upper], axis=1)


def whole(count):
    return [pl.BlockSpec(memory_space=pltpu.VMEM)] * count


def call(kernel, name, outs, scratch, scalars, args, weight, mib=24):
    specs = [pl.BlockSpec(memory_space=pltpu.SMEM)] * len(scalars) + whole(len(args))
    many = isinstance(outs, list)
    return pl.pallas_call(
        kernel,
        out_shape=outs,
        in_specs=specs,
        out_specs=whole(len(outs)) if many else whole(1)[0],
        scratch_shapes=scratch,
        compiler_params=pltpu.CompilerParams(vmem_limit_bytes=(56 if lax.axis_size("lon") > 8 else mib) * MIB),
        cost_estimate=pl.CostEstimate(
            flops=weight * 1_000_000, bytes_accessed=1_000, transcendentals=0
        ),
        name=name,
    )(*scalars, *args)


def split_outside(value):
    upper = lax.reduce_precision(value, exponent_bits=8, mantissa_bits=7)
    return upper.astype(BF16), (value - upper).astype(BF16)


def make_tables(plan, me):
    step = plan.lons_pad
    column = jnp.arange(plan.ring * step, dtype=jnp.int32)
    local_lon = column % step
    lon = (me ^ (column // step)) * plan.lons + local_lon
    row = jnp.arange(2 * plan.modes_pad, dtype=jnp.int32)
    wave = row % plan.modes_pad
    quarter = jnp.where(row >= plan.modes_pad, 0.5 * math.pi, 0.0).astype(F32)
    phase = wave[:, None] * lon[None, :] % plan.nlon
    table = jnp.cos(phase.astype(F32) * (2.0 * math.pi / plan.nlon) + quarter[:, None])
    live = (wave < plan.modes)[:, None] & (local_lon < plan.lons)[None, :]
    forward = lax.optimization_barrier(split_outside(jnp.where(live, table, 0.0)))
    return forward + (forward[0].T, forward[1].T)


def make_gain(plan, me, response):
    lane = jnp.arange(plan.lanes_pad, dtype=jnp.int32)
    whole_lanes = plan.full * plan.rows
    left = plan.full * plan.ring + (me * plan.left_lanes + lane - whole_lanes) // plan.rows
    variable = jnp.where(lane < whole_lanes, me * plan.full + lane // plan.rows, left)
    pick = (jnp.arange(plan.variables)[:, None] == variable[None, :]).astype(F32)
    gain = jnp.einsum("cm,cl->ml", response, pick, precision=lax.Precision.HIGHEST)
    weight = jnp.where(jnp.arange(plan.modes) == 0, 1.0, 2.0) / plan.nlon
    gain = gain * weight[:, None]
    return jnp.pad(gain, ((0, plan.modes_pad - plan.modes), (0, 0)))


def between_chips(pairs, ring):
    got = list(pairs)
    for k in sorted(range(1, ring // 2), reverse=True):
        got[k] = lax.ppermute(pairs[k], "lon", [(i, i ^ (2 * k)) for i in range(ring)])
    return got


def between_cores(got, ring):
    swap = [(i, i ^ 1) for i in range(ring)]
    return [*got, *(lax.ppermute(pair, "lon", swap) for pair in got)]


def after(values, *others):
    return lax.optimization_barrier((values, others))[0]


def local(
    analysis_fields,
    response_inphase,
    response_quadrature,
    entry_projection_matrix,
    exit_projection_matrix,
    radiance_op,
    inv_var,
    observed,
    cell_index,
    obs_mask,
):
    ring = lax.axis_size("lon")
    variables, rows, lons = analysis_fields.shape
    chunks = CHUNKS
    plan = Plan(variables, rows // chunks, lons, ring)
    chips = ring // 2
    pitch = plan.pitch
    parts, slots = cell_index.shape
    lon_at = lax.axis_index("lon")
    me = lon_at.astype(jnp.int32).reshape(1)
    state = jnp.transpose(analysis_fields, (2, 0, 1))

    def wire(count=1):
        return [jax.ShapeDtypeStruct((2 * count * plan.wire_rows, 128), F32)] * chips

    field = pltpu.VMEM((lons * pitch, 128), F32)
    bind = functools.partial

    blocks = call(
        bind(pack_kernel, plan, chunks), "pack_state", wire(chunks), [field], [me], [state], SHORT
    )
    circles = between_chips(blocks, ring)

    hidden = entry_projection_matrix.shape[1]
    stacked = [(hidden, 3 * pitch)] * 2 + [(pitch, 3 * pitch)] + [(2 * pitch, hidden)] * 2
    stacked += [(pitch, radiance_op.shape[1])] * 2
    *weights, op_hi, op_lo = call(
        bind(weights_kernel, plan),
        "weights",
        [jax.ShapeDtypeStruct(shape, BF16) for shape in stacked],
        [],
        [],
        [
            after(entry_projection_matrix, blocks[0]),
            exit_projection_matrix.T,
            radiance_op,
            inv_var[None, :],
        ],
        SHORT,
    )
    row, lon = cell_index // lons, cell_index % lons
    cell = row // plan.rows * plan.cells_pad + lon * plan.rows + row % plan.rows
    key = jnp.where(obs_mask > 0, cell, -1).astype(F32)
    sent = call(
        bind(observe_kernel, plan, parts),
        "pull_back",
        jax.ShapeDtypeStruct((parts * pitch, slots), F32),
        [],
        [],
        [op_hi, op_lo, key, observed.reshape(-1, slots)],
        SHORT,
    )
    arrived = lax.all_to_all(
        sent.reshape(parts, pitch, slots), ("lat", "lon"), split_axis=0, concat_axis=0, tiled=True
    ).reshape(parts * pitch, slots)

    tables = make_tables(plan, lon_at)
    gain_re = make_gain(plan, lon_at, response_inphase)
    gain_im = make_gain(plan, lon_at, response_quadrature)

    def apply_filter(name, imag, got, count, weight):
        columns = pltpu.VMEM((ring * plan.lons_pad, count * plan.lanes_pad), BF16)
        return call(
            bind(filter_kernel, plan, count),
            name,
            wire() * count,
            [columns, columns],
            [],
            [*tables, gain_re, imag, *got],
            weight,
        )

    circles = after(circles, sent, tables, gain_re, gain_im, weights)
    circles = between_cores(circles, ring)
    shifted = apply_filter("filter", gain_im, circles, chunks, W1)
    shifted = [between_chips(shifted[h * chips : (h + 1) * chips], ring) for h in range(chunks)]

    total_rows = -(-chunks * plan.cells_pad // CELL_TILE) * 2 * pitch
    sums = call(
        bind(collect_kernel, plan, chunks, parts),
        "collect",
        jax.ShapeDtypeStruct((pitch, chunks * plan.cells_pad), F32),
        [
            pltpu.VMEM((total_rows, 8 * slots), BF16),
            pltpu.VMEM((total_rows, CELL_TILE), F32),
        ],
        [],
        [arrived],
        SHORT,
    )
    d_mixed, d_circles, waits = [], [], sums
    for h in range(chunks):
        got = between_cores(after(shifted[h], waits), ring)
        out = call(
            bind(network_kernel, plan, h),
            "network",
            wire() + [jax.ShapeDtypeStruct((lons, variables, plan.rows), F32)],
            [field, pltpu.VMEM((pitch, plan.cells_pad), F32)],
            [me],
            [state, sums, *weights, *got],
            LONG,
        )
        waits = out[0]
        d_mixed.append(out[-1])
        d_circles.append(between_chips(out[:-1], ring))
    returned = []
    for h in range(chunks):
        got = between_cores(after(d_circles[h], waits), ring)
        weight = W2 if h > 0 else SHORT
        out = apply_filter("filter_transposed", -gain_im, got, 1, weight)
        waits = out[0]
        returned.append(between_chips(out, ring))
    arrivals = []
    for h in range(chunks):
        arrivals += between_cores(after(returned[h], waits), ring)
    gradient = call(
        bind(finish_kernel, plan, chunks),
        "finish",
        jax.ShapeDtypeStruct(state.shape, F32),
        [field] * chunks,
        [me],
        [*d_mixed, *arrivals],
        SHORT,
    )
    return jnp.transpose(gradient, (1, 2, 0))


def solution(mesh):
    return jax.shard_map(
        local,
        mesh=mesh,
        in_specs=(
            P(None, "lat", "lon"),
            P(),
            P(),
            P(),
            P(),
            P(),
            P(),
            P(None, ("lat", "lon"), None),
            P(("lat", "lon"), None),
            P(("lat", "lon"), None),
        ),
        out_specs=P(None, "lat", "lon"),
        check_vma=False,
    )
```
